32 devices in a mesh: row: 16 (over z, y, x), col: 2 (over core).
Axes of the slice: x: 2, y: 2, z: 4, core: 2. Of those that a mesh axis runs over, the one named last changes fastest.
Arguments:
- token_keys: bfloat16 [16384, 768], P(('row', 'col')), may hold values from -6 to 6
- token_values: bfloat16 [16384, 768], P(('row', 'col')), may hold values from -6 to 6
- token_queries: bfloat16 [16384, 768], P(('row', 'col')), may hold values from -6 to 6
- step_rates: float32 [16384], P(('row', 'col')), may hold values from 5e-05 to 0.0005
- fast_gate: float32 [768, 768], P('col'), may hold values from -0.21875 to 0.21875
- fast_up: float32 [768, 768], P('col'), may hold values from -0.21875 to 0.21875
- fast_down: float32 [768, 768], P('col'), may hold values from -0.21875 to 0.21875
- norm_gain: float32 [768], replicated, may hold values from 0.25 to 1.75
- proj_query: bfloat16 [768, 768], replicated, may hold values from -0.21875 to 0.21875
- proj_key: bfloat16 [768, 768], replicated, may hold values from -0.21875 to 0.21875
- proj_value: bfloat16 [768, 768], replicated, may hold values from -0.21875 to 0.21875
- head_temper: float32 [12], replicated, may hold values from 1 to 12
Outputs:
- attended: bfloat16 [16384, 768], P(('row', 'col'))
- new_gate: float32 [768, 768], P('col')
- new_up: float32 [768, 768], P('col')
- new_down: float32 [768, 768], P('col')
The draws below stay inside these ranges and needn't reach their ends.
All inputs are finite; a program needn't handle non-finite values.
Results may differ from the reference program's by a relative error of at most 0.035.
The reference program's roundings to bfloat16 on the way count: a program that leaves them out, or rounds other values in their place, can miss the bound.
Values may be sent and summed in bfloat16 or wider, within the bound.
A program may use at most 64 MiB of HBM per device.

```python
import math
import jax
import jax.numpy as jnp
from jax import lax

D = 768
H = 768
HEADS = 12
TOK_DEV = 512
HALF = 256
TOKENS = 16384


def draw_head_temper(key, part):
    first = jax.random.fold_in(key, 11)
    modest = jnp.exp(jax.random.uniform(first, (HEADS,), jnp.float32, jnp.log(1.0), jnp.log(4.0)))
    return modest


def levels(rng, dims, split, least, top_value):
    factor_of = 1.0
    for dim, shards_of in split:
        heights = jax.random.uniform(jax.random.fold_in(jax.random.fold_in(rng, 6), dim), (shards_of,), jnp.float32, least / len(split), top_value / len(split))
        factor_of = factor_of * jnp.repeat(jnp.exp(heights), dims[dim] // shards_of).reshape((-1,) + (1,) * (len(dims) - 1 - dim))
    return factor_of


def noise(rng, dims, scale, reach, shards=(), kind=jnp.bfloat16):
    entries = jax.random.normal(rng, dims, jnp.float32) * scale
    if len(shards) > 0:
        entries = levels(rng, dims, shards, -0.22, 0.18) * entries
    return jnp.clip(entries, min=-reach, max=reach).astype(kind)


def setup_inputs(seed: int = 0) -> dict:
    splits = jax.random.split(jax.random.key(seed), 13)
    token_keys = noise(splits[0], (TOKENS, D), 1.0, 6.0, ((0, 32),))
    token_values = noise(splits[1], (TOKENS, D), 1.0, 6.0, ((0, 32),))
    token_queries = noise(splits[2], (TOKENS, D), 1.0, 6.0, ((0, 32),))
    step_rates = jnp.clip(jnp.exp(math.log(0.0005) - 2.3025852 * jax.random.uniform(splits[3], (TOKENS,), jnp.float32) ** levels(splits[3], (TOKENS,), ((0, 32),), -0.2, 0.2)), 4.999999873689376e-05, 0.0005)
    fast_gate = noise(splits[4], (H, D), D ** -0.5, 0.21875, ((0, 2),), jnp.float32)
    fast_up = noise(splits[5], (H, D), D ** -0.5, 0.21875, ((0, 2),), jnp.float32)
    fast_down = noise(splits[6], (D, H), H ** -0.5, 0.21875, ((0, 2),), jnp.float32)
    norm_gain = jnp.clip(1.0 + 0.15 * jax.random.normal(splits[7], (D,), jnp.float32), 0.25, 1.75)
    proj_query = noise(splits[8], (D, D), D ** -0.5, 0.21875)
    proj_key = noise(splits[9], (D, D), D ** -0.5, 0.21875)
    proj_value = noise(splits[10], (D, D), D ** -0.5, 0.21875)
    head_temper = draw_head_temper(jax.random.fold_in(splits[12], 71), 0)
    return {"token_keys": token_keys, "token_values": token_values, "token_queries": token_queries, "step_rates": step_rates, "fast_gate": fast_gate, "fast_up": fast_up, "fast_down": fast_down, "norm_gain": norm_gain, "proj_query": proj_query, "proj_key": proj_key, "proj_value": proj_value, "head_temper": head_temper}


EPS_NORM = 1e-06

def dot_rows(left, right):
    return lax.dot_general(left, right, (((1,), (1,)), ((), ())), preferred_element_type=jnp.float32)

def dot_cols(left, right):
    return lax.dot_general(left, right, (((0,), (0,)), ((), ())), preferred_element_type=jnp.float32)

def fast_gradients(token_keys, token_values, step_rates, gate_b, up_b, down_b):
    pre_gate = dot_rows(token_keys, gate_b)
    pre_up = dot_rows(token_keys, up_b)
    sigmoid_gate = jax.nn.sigmoid(pre_gate)
    hidden = (pre_gate * sigmoid_gate * pre_up).astype(jnp.bfloat16)
    d_output = (-step_rates[:, None] * token_values.astype(jnp.float32)).astype(jnp.bfloat16)
    d_hidden = jnp.dot(d_output, down_b, preferred_element_type=jnp.float32)
    d_up = (d_hidden * pre_gate * sigmoid_gate).astype(jnp.bfloat16)
    d_gate = (d_hidden * pre_up * sigmoid_gate * (1.0 + pre_gate * (1.0 - sigmoid_gate))).astype(jnp.bfloat16)
    return (dot_cols(d_gate, token_keys), dot_cols(d_up, token_keys), dot_cols(d_output, hidden))

def renorm(weight, gradient):
    moved = weight - gradient
    keep = jnp.sqrt(lax.optimization_barrier(jnp.sum(weight * weight, axis=1, keepdims=True)))
    return moved * keep * lax.rsqrt(lax.optimization_barrier(jnp.sum(moved * moved, axis=1, keepdims=True)) + EPS_NORM)

def fast_apply(token_queries, gate_b, up_b, down_b):
    pre_gate = dot_rows(token_queries, gate_b)
    pre_up = dot_rows(token_queries, up_b)
    mixed = (pre_gate * jax.nn.sigmoid(pre_gate) * pre_up).astype(jnp.bfloat16)
    return dot_rows(mixed, down_b)

def normed_rows(fast_out, norm_gain):
    inverse = lax.rsqrt(lax.optimization_barrier(jnp.mean(fast_out * fast_out, axis=1, keepdims=True)) + EPS_NORM)
    return (fast_out * inverse * norm_gain[None, :]).astype(jnp.bfloat16)

def head_norm(projected, heads):
    count, features = projected.shape
    shaped = projected.reshape(count, heads, features // heads)
    shaped = shaped * lax.rsqrt(lax.optimization_barrier(jnp.mean(shaped * shaped, axis=2, keepdims=True)) + EPS_NORM)
    return shaped.reshape(count, features).astype(jnp.bfloat16)

def attend(q_rows, k_rows, v_rows, head_temper, half_span):
    heads = head_temper.shape[0]
    head_size = q_rows.shape[1] // heads
    query_count = q_rows.shape[0]
    key_count = k_rows.shape[0]
    offset = jnp.arange(key_count)[None, :] - half_span - jnp.arange(query_count)[:, None]
    inside = jnp.abs(offset) <= half_span

    def one_head(head):
        start = (head * head_size).astype(jnp.int32)
        query_h = lax.dynamic_slice_in_dim(q_rows, start, head_size, 1)
        key_h = lax.dynamic_slice_in_dim(k_rows, start, head_size, 1)
        value_h = lax.dynamic_slice_in_dim(v_rows, start, head_size, 1)
        scores = dot_rows(query_h, key_h) * (head_temper[head] / math.sqrt(head_size))
        scores = jnp.where(inside, scores, -1e+30)
        highest = lax.optimization_barrier(jnp.max(scores, axis=1, keepdims=True))
        weights = jnp.exp(scores - highest)
        weights = weights / lax.optimization_barrier(jnp.sum(weights, axis=1, keepdims=True))
        return jnp.dot(weights.astype(jnp.bfloat16), value_h, preferred_element_type=jnp.float32)
    stacked = lax.map(one_head, jnp.arange(heads, dtype=jnp.int32))
    return jnp.transpose(stacked, (1, 0, 2)).reshape(query_count, heads * head_size)

def reference(token_keys, token_values, token_queries, step_rates, fast_gate, fast_up, fast_down, norm_gain, proj_query, proj_key, proj_value, head_temper):
    blocks = TOKENS // TOK_DEV
    gate_b = fast_gate.astype(jnp.bfloat16)
    up_b = fast_up.astype(jnp.bfloat16)
    down_b = fast_down.astype(jnp.bfloat16)
    key_blocks = token_keys.reshape(blocks, TOK_DEV, D)
    value_blocks = token_values.reshape(blocks, TOK_DEV, D)
    rate_blocks = step_rates.reshape(blocks, TOK_DEV)

    def accumulate(carry, block_in):
        parts = fast_gradients(block_in[0], block_in[1], block_in[2], gate_b, up_b, down_b)
        return ((carry[0] + parts[0], carry[1] + parts[1], carry[2] + parts[2]), None)
    start_sums = (jnp.zeros((H, D), jnp.float32), jnp.zeros((H, D), jnp.float32), jnp.zeros((D, H), jnp.float32))
    sums, unused = lax.scan(accumulate, start_sums, (key_blocks, value_blocks, rate_blocks))
    new_gate = renorm(fast_gate, sums[0])
    new_up = renorm(fast_up, sums[1])
    new_down = renorm(fast_down, sums[2])
    fast_out = fast_apply(token_queries, new_gate.astype(jnp.bfloat16), new_up.astype(jnp.bfloat16), new_down.astype(jnp.bfloat16))
    normed = normed_rows(fast_out, norm_gain)
    query_n = head_norm(jnp.dot(normed, proj_query, preferred_element_type=jnp.float32), HEADS)
    key_n = head_norm(jnp.dot(normed, proj_key, preferred_element_type=jnp.float32), HEADS)
    value_b = jnp.dot(normed, proj_value, preferred_element_type=jnp.float32).astype(jnp.bfloat16)
    key_pad = jnp.concatenate([key_n[TOKENS - HALF:], key_n, key_n[:HALF]], axis=0)
    value_pad = jnp.concatenate([value_b[TOKENS - HALF:], value_b, value_b[:HALF]], axis=0)

    def one_block(block):
        start = (block * TOK_DEV).astype(jnp.int32)
        q_rows = lax.dynamic_slice_in_dim(query_n, start, TOK_DEV, 0)
        k_rows = lax.dynamic_slice_in_dim(key_pad, start, TOK_DEV + 2 * HALF, 0)
        v_rows = lax.dynamic_slice_in_dim(value_pad, start, TOK_DEV + 2 * HALF, 0)
        return attend(q_rows, k_rows, v_rows, head_temper, HALF)
    attended = lax.map(one_block, jnp.arange(blocks, dtype=jnp.int32))
    return (attended.reshape(TOKENS, D).astype(jnp.bfloat16), new_gate, new_up, new_down)
```

```python
import functools
import math

import jax
import jax.numpy as jnp
from jax import lax
from jax.experimental import pallas as pl
from jax.experimental.pallas import tpu as pltpu
from jax.sharding import PartitionSpec as P

EPS_NORM = 1e-06
MESH = pl.DeviceIdType.MESH
VMEM = pltpu.VMEM
PART = 256
LIMIT = 50 * 1024 * 1024


def dot_rows(left, right):
    return lax.dot_general(
        left, right, (((1,), (1,)), ((), ())), preferred_element_type=jnp.float32
    )


def dot_cols(left, right):
    return lax.dot_general(
        left, right, (((0,), (0,)), ((), ())), preferred_element_type=jnp.float32
    )


def exchange_kernel(n_row, n_col, gate, up, down, queries, weights, halo, w_send, w_recv, h_send, h_recv):
    row, col = lax.axis_index("row"), lax.axis_index("col")
    total = n_row * n_col
    place = row * n_col + col
    after, before = lax.rem(place + 1, total), lax.rem(place + total - 1, total)
    after_id = (after // n_col, lax.rem(after, n_col))
    before_id = (before // n_col, lax.rem(before, n_col))
    peers = [(row, lax.rem(col + step, n_col)) for step in range(1, n_col)]
    barrier = pltpu.get_barrier_semaphore()
    for target in peers + [after_id, before_id]:
        pl.semaphore_signal(barrier, inc=1, device_id=target, device_id_type=MESH)
    for m, source in enumerate((gate, up, down)):
        weights[m, col] = source[...].astype(jnp.bfloat16)
    pl.semaphore_wait(barrier, n_col + 1)
    copies = []
    for m in range(3):
        for step, peer in enumerate(peers):
            copies.append(
                pltpu.make_async_remote_copy(
                    src_ref=weights.at[m, col],
                    dst_ref=weights.at[m, col],
                    send_sem=w_send.at[m, step],
                    recv_sem=w_recv.at[m, step],
                    device_id=peer,
                    device_id_type=MESH,
                )
            )
    half = halo.shape[1]
    count = queries.shape[0]
    copies.append(
        pltpu.make_async_remote_copy(
            src_ref=queries.at[pl.ds(count - half, half)],
            dst_ref=halo.at[0],
            send_sem=h_send.at[0],
            recv_sem=h_recv.at[0],
            device_id=after_id,
            device_id_type=MESH,
        )
    )
    copies.append(
        pltpu.make_async_remote_copy(
            src_ref=queries.at[pl.ds(0, half)],
            dst_ref=halo.at[1],
            send_sem=h_send.at[1],
            recv_sem=h_recv.at[1],
            device_id=before_id,
            device_id_type=MESH,
        )
    )
    for copy in copies:
        copy.start()
    for copy in copies:
        copy.wait()


def exchange(n_row, n_col, gate, up, down, queries):
    rows, features = gate.shape
    half = queries.shape[0] // 2
    return pl.pallas_call(
        functools.partial(exchange_kernel, n_row, n_col),
        out_shape=(
            jax.ShapeDtypeStruct((3, n_col, rows, features), jnp.bfloat16),
            jax.ShapeDtypeStruct((2, half, features), jnp.bfloat16),
        ),
        in_specs=[pl.BlockSpec(memory_space=VMEM)] * 3 + [pl.BlockSpec(memory_space=pl.ANY)],
        out_specs=(pl.BlockSpec(memory_space=VMEM), pl.BlockSpec(memory_space=pl.ANY)),
        scratch_shapes=[
            pltpu.SemaphoreType.DMA((3, max(n_col - 1, 1))),
            pltpu.SemaphoreType.DMA((3, max(n_col - 1, 1))),
            pltpu.SemaphoreType.DMA((2,)),
            pltpu.SemaphoreType.DMA((2,)),
        ],
        compiler_params=pltpu.CompilerParams(
            collective_id=0, has_side_effects=True, vmem_limit_bytes=LIMIT
        ),
        name="exchange",
    )(gate, up, down, queries)


def gradient_kernel(n_col, keys, values, rates, weights, out, hidden, d_output, d_up, d_gate):
    chunk = keys.shape[0] // 2
    rows = weights.shape[1] // n_col
    parts = keys.shape[1] // PART
    for start in range(0, keys.shape[0], chunk):
        span = pl.ds(start, chunk)
        token = keys[span, :]
        pre_gate = dot_rows(token, weights[0])
        pre_up = dot_rows(token, weights[1])
        d_out = (-rates[span, :] * values[span, :].astype(jnp.float32)).astype(jnp.bfloat16)
        d_output[span, :] = d_out
        d_hidden = jnp.dot(d_out, weights[2], preferred_element_type=jnp.float32)
        sig = jax.nn.sigmoid(pre_gate)
        silu = pre_gate * sig
        hidden[span, :] = (silu * pre_up).astype(jnp.bfloat16)
        d_up[span, :] = (d_hidden * silu).astype(jnp.bfloat16)
        d_gate[span, :] = (d_hidden * pre_up * sig * (1.0 + pre_gate * (1.0 - sig))).astype(jnp.bfloat16)
    for m, (left, right) in enumerate(((d_gate, keys), (d_up, keys), (d_output, hidden))):
        turned = left[...]
        for p in range(parts):
            summed = dot_cols(turned, right[:, p * PART : (p + 1) * PART]).astype(jnp.bfloat16)
            for c in range(n_col):
                out[p, c, m * rows : (m + 1) * rows, :] = summed[c * rows : (c + 1) * rows, :]


def gradients(n_col, keys, values, rates, weights):
    tokens, features = keys.shape
    rows = weights.shape[1] // n_col
    parts = features // PART
    return pl.pallas_call(
        functools.partial(gradient_kernel, n_col),
        out_shape=jax.ShapeDtypeStruct((parts, n_col, 3 * rows, PART), jnp.bfloat16),
        in_specs=[pl.BlockSpec(memory_space=VMEM)] * 4,
        out_specs=pl.BlockSpec(memory_space=VMEM),
        scratch_shapes=[VMEM((tokens, features), jnp.bfloat16)] * 4,
        compiler_params=pltpu.CompilerParams(vmem_limit_bytes=LIMIT),
        cost_estimate=pl.CostEstimate(
            flops=12 * tokens * features * features, bytes_accessed=9 * 2**20, transcendentals=0
        ),
        name="gradients",
    )(keys, values, rates, weights)


def update_kernel(
    n_row, n_col, bits, grads, gate, up, down, out,
    held, from_col, *rest,
):
    landing, (total, fast, c_send, c_recv, r_send, r_recv, g_send, g_recv, o_send, o_recv, f_sem) = (
        rest[:bits], rest[bits:]
    )
    row, col = lax.axis_index("row"), lax.axis_index("col")
    parts = grads.shape[0]
    unit = grads.shape[-2]
    mine = [lax.rem(row // (1 << b), 2) for b in range(bits)]
    peers = [(row, lax.rem(col + step, n_col)) for step in range(1, n_col)]
    partners = [(row + (1 - 2 * mine[b]) * (1 << b), col) for b in range(bits)]

    barrier = pltpu.get_barrier_semaphore()
    for target in peers + partners:
        pl.semaphore_signal(barrier, inc=1, device_id=target, device_id_type=MESH)
    rows = gate.shape[0]
    fills = [
        pltpu.make_async_copy(source, fast.at[pl.ds(m * rows, rows)], f_sem.at[m])
        for m, source in enumerate((gate, up, down))
    ]
    for fill in fills:
        fill.start()
    pl.semaphore_wait(barrier, len(peers) + len(partners))

    def planes(fixed):
        return tuple(fixed.get(b, slice(None)) for b in reversed(range(bits)))

    free = min(3, bits)

    def order(p):
        return [(p + s) % free for s in range(free)] + list(range(free, bits))

    first = {}
    for p in range(parts):
        for step, peer in enumerate(peers):
            first[p, step] = pltpu.make_async_remote_copy(
                src_ref=grads.at[p, peer[1]],
                dst_ref=from_col.at[step, p],
                send_sem=c_send.at[p, step],
                recv_sem=c_recv.at[p, step],
                device_id=peer,
                device_id_type=MESH,
            )
            first[p, step].start()

    halvings = {}

    def halve(p, s):
        b = order(p)[s]
        fixed = {order(p)[t]: mine[order(p)[t]] for t in range(s)}
        fixed[b] = 1 - mine[b]
        halvings[p, s] = pltpu.make_async_remote_copy(
            src_ref=held.at[(p,) + planes(fixed)],
            dst_ref=landing[s].at[p],
            send_sem=r_send.at[p, s],
            recv_sem=r_recv.at[p, s],
            device_id=partners[b],
            device_id_type=MESH,
        )
        halvings[p, s].start()

    for p in range(parts):
        for step in range(len(peers)):
            first[p, step].wait_recv()
        summed = grads[p, col].astype(jnp.float32)
        for step in range(len(peers)):
            summed = summed + from_col[step, p].astype(jnp.float32)
        held[p] = summed.astype(jnp.bfloat16)
        halve(p, 0)
    for s in range(bits):
        for p in range(parts):
            halvings[p, s].wait_recv()
            fixed = {order(p)[t]: mine[order(p)[t]] for t in range(s + 1)}
            index = (p,) + planes(fixed)
            summed = held[index].astype(jnp.float32) + landing[s][p].astype(jnp.float32)
            if s < bits - 1:
                held[index] = summed.astype(jnp.bfloat16)
                halve(p, s + 1)
            else:
                total[:, p * PART : (p + 1) * PART] = summed

    for fill in fills:
        fill.wait()
    if unit % 8 == 0:
        old = fast[pl.ds(pl.multiple_of(row * unit, 8), unit), :]
    else:
        old = sum(
            jnp.where(row == r, fast[r * unit : (r + 1) * unit, :], 0.0) for r in range(n_row)
        )
    moved = old - total[...]
    keep = jnp.sqrt(jnp.sum(old * old, axis=1, keepdims=True))
    new = moved * keep * lax.rsqrt(jnp.sum(moved * moved, axis=1, keepdims=True) + EPS_NORM)
    own = planes({b: mine[b] for b in range(bits)})
    doublings, handed = {}, {}

    def double(p, s):
        b = order(p)[s]
        part = (p, col) + planes({order(p)[t]: mine[order(p)[t]] for t in range(s + 1)})
        doublings[p, s] = pltpu.make_async_remote_copy(
            src_ref=out.at[part],
            dst_ref=out.at[part],
            send_sem=g_send.at[p, s],
            recv_sem=g_recv.at[p, s],
            device_id=partners[b],
            device_id_type=MESH,
        )
        doublings[p, s].start()

    for p in range(parts):
        out[(p, col) + own] = new[:, p * PART : (p + 1) * PART].astype(jnp.bfloat16)
        double(p, bits - 1)
    for s in reversed(range(bits)):
        for p in range(parts):
            doublings[p, s].wait_recv()
            if s > 0:
                double(p, s - 1)
            else:
                for step, peer in enumerate(peers):
                    handed[p, step] = pltpu.make_async_remote_copy(
                        src_ref=out.at[p, col],
                        dst_ref=out.at[p, col],
                        send_sem=o_send.at[p, step],
                        recv_sem=o_recv.at[p, step],
                        device_id=peer,
                        device_id_type=MESH,
                    )
                    handed[p, step].start()
    for copy in handed.values():
        copy.wait_recv()
    for group in (first, halvings, doublings, handed):
        for copy in group.values():
            copy.wait_send()


def update(n_row, n_col, grads, gate, up, down):
    parts, _, stacked, width = grads.shape
    bits = n_row.bit_length() - 1
    unit = stacked // n_row
    block = (2,) * bits + (unit, width)
    grads = grads.reshape((parts, n_col) + block)
    features = gate.shape[1]
    step = max(n_col - 1, 1)
    dma = pltpu.SemaphoreType.DMA
    landing = [VMEM((parts,) + (2,) * (bits - 1 - s) + (unit, width), jnp.bfloat16) for s in range(bits)]
    new = pl.pallas_call(
        functools.partial(update_kernel, n_row, n_col, bits),
        out_shape=jax.ShapeDtypeStruct(grads.shape, jnp.bfloat16),
        in_specs=[pl.BlockSpec(memory_space=VMEM)] + [pl.BlockSpec(memory_space=pl.ANY)] * 3,
        out_specs=pl.BlockSpec(memory_space=VMEM),
        scratch_shapes=[
            VMEM((parts,) + block, jnp.bfloat16),
            VMEM((step, parts) + block, jnp.bfloat16),
            *landing,
            VMEM((unit, features), jnp.float32),
            VMEM((stacked, features), jnp.float32),
            dma((parts, step)),
            dma((parts, step)),
            dma((parts, bits)),
            dma((parts, bits)),
            dma((parts, bits)),
            dma((parts, bits)),
            dma((parts, step)),
            dma((parts, step)),
            dma((3,)),
        ],
        compiler_params=pltpu.CompilerParams(
            collective_id=1, has_side_effects=True, vmem_limit_bytes=LIMIT
        ),
        name="update",
    )(grads, gate, up, down)
    return new.reshape(parts, n_col, stacked, width)


def attend_kernel(
    n_col, heads, temper, queries, halo, weights, gain, proj_q, proj_k, proj_v,
    attended, new_gate, new_up, new_down, query_n, key_n, value_b, bias,
):
    parts = weights.shape[0]
    rows = weights.shape[2] // 3
    tokens, features = queries.shape
    half = tokens // 2
    size = features // heads
    col = lax.axis_index("col")
    for m, target in enumerate((new_gate, new_up, new_down)):
        for p in range(parts):
            target[:, p * PART : (p + 1) * PART] = weights[p, col, m * rows : (m + 1) * rows, :].astype(jnp.float32)

    def whole(m, p):
        return jnp.concatenate(
            [weights[p, c, m * rows : (m + 1) * rows, :] for c in range(n_col)], axis=0
        )

    def apply(m, left):
        return sum(dot_rows(left[:, p * PART : (p + 1) * PART], whole(m, p)) for p in range(parts))

    group_r = lax.broadcasted_iota(jnp.int32, (PART, PART), 0) // size
    group_c = lax.broadcasted_iota(jnp.int32, (PART, PART), 1) // size
    same = jnp.where(group_r == group_c, 1.0 / size, 0.0).astype(jnp.bfloat16)

    def head_norm(projected):
        pieces = []
        for p in range(parts):
            piece = projected[:, p * PART : (p + 1) * PART]
            square = piece * piece
            top = square.astype(jnp.bfloat16)
            rest = (square - top.astype(jnp.float32)).astype(jnp.bfloat16)
            mean = jnp.dot(top, same, preferred_element_type=jnp.float32) + jnp.dot(
                rest, same, preferred_element_type=jnp.float32
            )
            pieces.append((piece * lax.rsqrt(mean + EPS_NORM)).astype(jnp.bfloat16))
        return jnp.concatenate(pieces, axis=1)

    def project(normed, proj):
        return jnp.dot(normed, proj[...], preferred_element_type=jnp.float32)

    for own in (True, False):
        tokens_in = queries[...] if own else jnp.concatenate([halo[0], halo[1]], axis=0)
        pre_gate = apply(0, tokens_in)
        pre_up = apply(1, tokens_in)
        mixed = (pre_gate * jax.nn.sigmoid(pre_gate) * pre_up).astype(jnp.bfloat16)
        fast_out = apply(2, mixed)
        inverse = lax.rsqrt(jnp.mean(fast_out * fast_out, axis=1, keepdims=True) + EPS_NORM)
        normed = (fast_out * inverse * gain[...]).astype(jnp.bfloat16)
        keys = head_norm(project(normed, proj_k))
        values = project(normed, proj_v).astype(jnp.bfloat16)
        if own:
            query_n[...] = head_norm(project(normed, proj_q))
            key_n[half : half + tokens, :] = keys
            value_b[half : half + tokens, :] = values
        else:
            key_n[0:half, :] = keys[:half]
            value_b[0:half, :] = values[:half]
            key_n[half + tokens :, :] = keys[half:]
            value_b[half + tokens :, :] = values[half:]

    at = lax.broadcasted_iota(jnp.int32, (half, 3 * half), 1) - lax.broadcasted_iota(
        jnp.int32, (half, 3 * half), 0
    )
    bias[...] = jnp.where((at >= 0) & (at <= 2 * half), 0.0, -1e30)
    pair = 128 // size
    lane = lax.broadcasted_iota(jnp.int32, (half, 128), 1) // size
    ones = jnp.ones((3 * half, 128), jnp.bfloat16)

    def one_pair(j, carry):
        lanes = pl.ds(pl.multiple_of(j * 128, 128), 128)
        for block in range(2):
            span = pl.ds(block * half, half)
            window = pl.ds(block * half, 3 * half)
            query = query_n[span, lanes]
            key = key_n[window, lanes]
            value = jnp.concatenate([value_b[window, lanes], ones], axis=1)
            result = jnp.zeros((half, 128), jnp.float32)
            for h in range(pair):
                scale = temper[j * pair + h] * (math.log2(math.e) / math.sqrt(size))
                scores = dot_rows(jnp.where(lane == h, query, jnp.zeros_like(query)), key) + bias[...]
                highest = jnp.max(scores, axis=1, keepdims=True)
                weight = jnp.exp2((scores - highest) * scale).astype(jnp.bfloat16)
                both = jnp.dot(weight, value, preferred_element_type=jnp.float32)
                result = jnp.where(lane == h, both[:, :128] / both[:, 128:], result)
            attended[span, lanes] = result.astype(jnp.bfloat16)
        return carry

    lax.fori_loop(0, features // 128, one_pair, 0)


def attend(n_col, queries, halo, weights, gain, proj_q, proj_k, proj_v, temper):
    tokens, features = queries.shape
    rows = weights.shape[2] // 3
    half = tokens // 2
    vmem = pl.BlockSpec(memory_space=VMEM)
    square = jax.ShapeDtypeStruct((rows, features), jnp.float32)
    return pl.pallas_call(
        functools.partial(attend_kernel, n_col, temper.shape[0]),
        out_shape=(jax.ShapeDtypeStruct((tokens, features), jnp.bfloat16), square, square, square),
        in_specs=[pl.BlockSpec(memory_space=pltpu.SMEM)] + [vmem] * 7,
        out_specs=(vmem,) * 4,
        scratch_shapes=[
            VMEM((tokens, features), jnp.bfloat16),
            VMEM((2 * tokens, features), jnp.bfloat16),
            VMEM((2 * tokens, features), jnp.bfloat16),
            VMEM((half, 3 * half), jnp.float32),
        ],
        compiler_params=pltpu.CompilerParams(vmem_limit_bytes=LIMIT),
        name="attend",
    )(temper, queries, halo, weights, gain[None, :], proj_q, proj_k, proj_v)


def per_device(
    n_row,
    n_col,
    token_keys,
    token_values,
    token_queries,
    step_rates,
    fast_gate,
    fast_up,
    fast_down,
    norm_gain,
    proj_query,
    proj_key,
    proj_value,
    head_temper,
):
    weights, halo = exchange(n_row, n_col, fast_gate, fast_up, fast_down, token_queries)
    weights = weights.reshape(3, -1, fast_gate.shape[1])
    grads = gradients(n_col, token_keys, token_values, step_rates[:, None], weights)
    new = update(n_row, n_col, grads, fast_gate, fast_up, fast_down)
    return attend(
        n_col, token_queries, halo, new, norm_gain, proj_query, proj_key, proj_value, head_temper
    )


def solution(mesh):
    placed = (
        P(("row", "col"), None),
        P(("row", "col"), None),
        P(("row", "col"), None),
        P(("row", "col")),
        P("col", None),
        P("col", None),
        P("col", None),
        P(),
        P(),
        P(),
        P(),
        P(),
    )
    return jax.shard_map(
        functools.partial(per_device, mesh.shape["row"], mesh.shape["col"]),
        mesh=mesh,
        in_specs=placed,
        out_specs=(P(("row", "col"), None), P("col", None), P("col", None), P("col", None)),
        check_vma=False,
    )
```

```python
import functools
import math

import jax
import jax.numpy as jnp
from jax import lax
from jax.experimental import pallas as pl
from jax.experimental.pallas import tpu as pltpu
from jax.sharding import PartitionSpec as P

EPS_NORM = 1e-06
MESH = pl.DeviceIdType.MESH
VMEM = pltpu.VMEM
PART = 256
WIDTH = 128
LIMIT = 60 * 1024 * 1024


def dot_rows(left, right):
    return lax.dot_general(
        left, right, (((1,), (1,)), ((), ())), preferred_element_type=jnp.float32
    )


def update_kernel(
    n_row, n_col, bits,
    gate, up, down, keys_in, values_in, queries, rates,
    out_far, halo,
    out, fast, weights, keys, values, left, hidden, grads, held, from_col, *rest,
):
    landing, (
        total, f_sem, t_sem, x_sem, w_send, w_recv, h_send, h_recv,
        c_send, c_recv, r_send, r_recv, g_send, g_recv, o_send, o_recv,
    ) = rest[:bits], rest[bits:]
    row, col = lax.axis_index("row"), lax.axis_index("col")
    parts = grads.shape[0]
    unit = total.shape[0]
    rows = gate.shape[0]
    count = keys.shape[0]
    half = count // 2
    devices = n_row * n_col
    place = row * n_col + col
    after, before = lax.rem(place + 1, devices), lax.rem(place + devices - 1, devices)
    after_id = (after // n_col, lax.rem(after, n_col))
    before_id = (before // n_col, lax.rem(before, n_col))
    mine = [lax.rem(row // (1 << b), 2) for b in range(bits)]
    peers = [(row, lax.rem(col + step, n_col)) for step in range(1, n_col)]
    partners = [(row + (1 - 2 * mine[b]) * (1 << b), col) for b in range(bits)]

    barrier = pltpu.get_barrier_semaphore()
    everyone = peers + [after_id, before_id] + partners
    for target in everyone:
        pl.semaphore_signal(barrier, inc=1, device_id=target, device_id_type=MESH)
    fills = [
        pltpu.make_async_copy(source, fast.at[pl.ds(m * rows, rows)], f_sem.at[m])
        for m, source in enumerate((gate, up, down))
    ]
    tokens = [
        pltpu.make_async_copy(keys_in, keys, t_sem.at[0]),
        pltpu.make_async_copy(values_in, values, t_sem.at[1]),
    ]
    for copy in (fills[0], tokens[0], fills[1], fills[2], tokens[1]):
        copy.start()

    def remote(source, target, send, recv, device):
        copy = pltpu.make_async_remote_copy(
            src_ref=source, dst_ref=target, send_sem=send, recv_sem=recv,
            device_id=device, device_id_type=MESH,
        )
        copy.start()
        return copy

    given = {}
    for m in range(3):
        fills[m].wait()
        weights[m, col] = fast[m * rows : (m + 1) * rows, :].astype(jnp.bfloat16)
        if m == 0:
            pl.semaphore_wait(barrier, len(everyone))
        for step, peer in enumerate(peers):
            given[m, step] = remote(
                weights.at[m, col], weights.at[m, col], w_send.at[m, step], w_recv.at[m, step], peer
            )
    edges = {
        0: remote(queries.at[pl.ds(count - half, half)], halo.at[0], h_send.at[0], h_recv.at[0], after_id),
        1: remote(queries.at[pl.ds(0, half)], halo.at[1], h_send.at[1], h_recv.at[1], before_id),
    }

    def ready(m):
        for step in range(len(peers)):
            given[m, step].wait_recv()
        return weights[m].reshape(n_col * rows, weights.shape[3])

    for token in tokens:
        token.wait()
    token = keys[...]
    size = min(128, count)
    same = lax.broadcasted_iota(jnp.int32, (size, size), 0) == lax.broadcasted_iota(
        jnp.int32, (size, size), 1
    )
    rate_column = jnp.concatenate(
        [
            jnp.sum(
                jnp.where(same, rates[start : start + size][None, :], 0.0), axis=1, keepdims=True
            )
            for start in range(0, count, size)
        ],
        axis=0,
    )
    d_out = (-rate_column * values[...].astype(jnp.float32)).astype(jnp.bfloat16)
    left[2] = d_out.T
    pre_gate = dot_rows(token, ready(0))
    pre_up = dot_rows(token, ready(1))
    sig = jax.nn.sigmoid(pre_gate)
    silu = pre_gate * sig
    hidden[...] = (silu * pre_up).astype(jnp.bfloat16)
    d_hidden = jnp.dot(d_out, ready(2), preferred_element_type=jnp.float32)
    left[1] = (d_hidden * silu).astype(jnp.bfloat16).T
    left[0] = (d_hidden * pre_up * sig * (1.0 + pre_gate * (1.0 - sig))).astype(jnp.bfloat16).T

    def planes(fixed):
        return tuple(fixed.get(b, slice(None)) for b in reversed(range(bits)))

    free = min(3, bits)

    def order(p):
        return [(p + s) % free for s in range(free)] + list(range(free, bits))

    def chosen(p, steps):
        return {b: mine[b] for b in order(p)[:steps]}

    first, halvings = {}, {}

    def halve(p, s):
        b = order(p)[s]
        halvings[p, s] = remote(
            held.at[(p,) + planes({**chosen(p, s), b: 1 - mine[b]})],
            landing[s].at[p], r_send.at[p, s], r_recv.at[p, s], partners[b],
        )

    def gather_columns(p):
        for step in range(len(peers)):
            first[p, step].wait_recv()
        summed = grads[p, col].astype(jnp.float32)
        for step in range(len(peers)):
            summed = summed + from_col[step, p].astype(jnp.float32)
        for r in range(n_row):
            place_r = tuple((r >> b) & 1 for b in reversed(range(bits)))
            held[(p,) + place_r] = summed[r * unit : (r + 1) * unit, :].astype(jnp.bfloat16)
        halve(p, 0)

    joined = PART // WIDTH
    for start in range(0, parts, joined):
        for m, right in enumerate((keys, keys, hidden)):
            summed = jnp.dot(
                left[m], right[:, start * WIDTH : (start + joined) * WIDTH],
                preferred_element_type=jnp.float32,
            ).astype(jnp.bfloat16)
            for p in range(joined):
                for c in range(n_col):
                    grads[start + p, c, m * rows : (m + 1) * rows, :] = summed[
                        c * rows : (c + 1) * rows, p * WIDTH : (p + 1) * WIDTH
                    ]
        for p in range(start, start + joined):
            for step, peer in enumerate(peers):
                first[p, step] = remote(
                    grads.at[p, peer[1]], from_col.at[step, p],
                    c_send.at[p, step], c_recv.at[p, step], peer,
                )
        for p in range(start - joined, start):
            if p >= 0:
                gather_columns(p)
    for p in range(parts - joined, parts):
        gather_columns(p)
    for s in range(bits):
        for p in range(parts):
            halvings[p, s].wait_recv()
            index = (p,) + planes(chosen(p, s + 1))
            summed = held[index].astype(jnp.float32) + landing[s][p].astype(jnp.float32)
            if s < bits - 1:
                held[index] = summed.astype(jnp.bfloat16)
                halve(p, s + 1)
            else:
                total[:, p * WIDTH : (p + 1) * WIDTH] = summed

    if unit % 8 == 0:
        old = fast[pl.ds(pl.multiple_of(row * unit, 8), unit), :]
    else:
        old = sum(
            jnp.where(row == r, fast[r * unit : (r + 1) * unit, :], 0.0) for r in range(n_row)
        )
    moved = old - total[...]
    keep = jnp.sqrt(jnp.sum(old * old, axis=1, keepdims=True))
    new = moved * keep * lax.rsqrt(jnp.sum(moved * moved, axis=1, keepdims=True) + EPS_NORM)
    doublings, handed = {}, {}

    def double(p, s):
        part = (p, col) + planes(chosen(p, s + 1))
        doublings[p, s] = remote(
            out.at[part], out.at[part], g_send.at[p, s], g_recv.at[p, s], partners[order(p)[s]]
        )

    def hand(p, side, value):
        part = (p, col) + planes({order(p)[0]: value})
        for step, peer in enumerate(peers):
            handed[p, side, step] = remote(
                out.at[part], out.at[part], o_send.at[p, side, step], o_recv.at[p, side, step], peer
            )

    leaving = []

    def leave(p, step):
        giver = lax.rem(col + n_col - step, n_col)
        copy = pltpu.make_async_copy(out.at[p, giver], out_far.at[p, giver], x_sem.at[p, step])
        copy.start()
        leaving.append(copy)

    for p in range(parts):
        out[(p, col) + planes(chosen(p, bits))] = new[:, p * WIDTH : (p + 1) * WIDTH].astype(jnp.bfloat16)
        double(p, bits - 1)
    for s in reversed(range(bits)):
        for p in range(parts):
            doublings[p, s].wait_recv()
            if s > 0:
                double(p, s - 1)
            if s == 1:
                hand(p, 0, mine[order(p)[0]])
            if s == 0:
                hand(p, 1, 1 - mine[order(p)[0]])
                leave(p, 0)
    for p in range(parts):
        for step in range(len(peers)):
            for side in range(2):
                handed[p, side, step].wait_recv()
            leave(p, step + 1)
    for copy in edges.values():
        copy.wait_recv()
    for copy in leaving:
        copy.wait()
    for group in (given, edges, first, halvings, doublings, handed):
        for copy in group.values():
            copy.wait_send()


def update(n_row, n_col, gate, up, down, keys, values, queries, rates):
    rows, features = gate.shape
    tokens = keys.shape[0]
    parts = features // WIDTH
    stacked = 3 * rows
    bits = n_row.bit_length() - 1
    unit = stacked // n_row
    block = (2,) * bits + (unit, WIDTH)
    step = max(n_col - 1, 1)
    dma = pltpu.SemaphoreType.DMA
    landing = [VMEM((parts,) + (2,) * (bits - 1 - s) + (unit, WIDTH), jnp.bfloat16) for s in range(bits)]
    new, halo = pl.pallas_call(
        functools.partial(update_kernel, n_row, n_col, bits),
        out_shape=(
            jax.ShapeDtypeStruct((parts, n_col) + block, jnp.bfloat16),
            jax.ShapeDtypeStruct((2, tokens // 2, features), jnp.bfloat16),
        ),
        in_specs=[pl.BlockSpec(memory_space=pl.ANY)] * 6 + [pl.BlockSpec(memory_space=VMEM)],
        out_specs=(pl.BlockSpec(memory_space=pl.ANY), pl.BlockSpec(memory_space=pl.ANY)),
        scratch_shapes=[
            VMEM((parts, n_col) + block, jnp.bfloat16),
            VMEM((stacked, features), jnp.float32),
            VMEM((3, n_col, rows, features), jnp.bfloat16),
            VMEM((tokens, features), jnp.bfloat16),
            VMEM((tokens, features), jnp.bfloat16),
            VMEM((3, features, tokens), jnp.bfloat16),
            VMEM((tokens, features), jnp.bfloat16),
            VMEM((parts, n_col, stacked, WIDTH), jnp.bfloat16),
            VMEM((parts,) + block, jnp.bfloat16),
            VMEM((step, parts, stacked, WIDTH), jnp.bfloat16),
            *landing,
            VMEM((unit, features), jnp.float32),
            dma((3,)),
            dma((2,)),
            dma((parts, n_col)),
            dma((3, step)),
            dma((3, step)),
            dma((2,)),
            dma((2,)),
            dma((parts, step)),
            dma((parts, step)),
            dma((parts, bits)),
            dma((parts, bits)),
            dma((parts, bits)),
            dma((parts, bits)),
            dma((parts, 2, step)),
            dma((parts, 2, step)),
        ],
        compiler_params=pltpu.CompilerParams(
            collective_id=0, has_side_effects=True, vmem_limit_bytes=LIMIT
        ),
        cost_estimate=pl.CostEstimate(
            flops=12 * tokens * features * features, bytes_accessed=12 * 2**20, transcendentals=0
        ),
        name="update",
    )(gate, up, down, keys, values, queries, rates)
    return new.reshape(parts, n_col, stacked, WIDTH), halo


def attend_kernel(
    n_col, heads, temper, queries_in, halo_in, weights_in, gain, proj_q_in, proj_k_in, proj_v_in,
    attended, new_gate, new_up, new_down,
    queries, halo, weights, proj, wide, query_n, key_n, value_b, bias, in_sem, w_sem, p_sem, n_sem,
):
    rows = weights.shape[3]
    tokens, features = queries.shape
    parts = features // PART
    joined = PART // WIDTH
    half = tokens // 2
    size = features // heads
    col = lax.axis_index("col")
    proj_q, proj_k, proj_v = 0, 1, 2
    token_fills = [
        pltpu.make_async_copy(queries_in, queries, in_sem.at[0]),
        pltpu.make_async_copy(halo_in, halo, in_sem.at[1]),
    ]
    weight_fills = [
        pltpu.make_async_copy(
            weights_in.at[:, :, pl.ds(m * rows, rows), :], weights.at[m], w_sem.at[m]
        )
        for m in range(3)
    ]
    proj_fills = [
        pltpu.make_async_copy(source, proj.at[i], p_sem.at[i])
        for i, source in enumerate((proj_q_in, proj_k_in, proj_v_in))
    ]
    for fill in (
        token_fills[0], *weight_fills, proj_fills[1], proj_fills[2], proj_fills[0], token_fills[1]
    ):
        fill.start()
    stores = [
        pltpu.make_async_copy(wide.at[m], target, n_sem.at[m])
        for m, target in enumerate((new_gate, new_up, new_down))
    ]

    def whole(m, p):
        return jnp.concatenate(
            [
                jnp.concatenate([weights[m, p * joined + i, c] for i in range(joined)], axis=1)
                for c in range(n_col)
            ],
            axis=0,
        )

    def apply(m, left):
        return sum(dot_rows(left[:, p * PART : (p + 1) * PART], whole(m, p)) for p in range(parts))

    group_r = lax.broadcasted_iota(jnp.int32, (PART, PART), 0) // size
    group_c = lax.broadcasted_iota(jnp.int32, (PART, PART), 1) // size
    same = jnp.where(group_r == group_c, 1.0 / size, 0.0).astype(jnp.bfloat16)

    def head_norm(projected):
        pieces = []
        for p in range(parts):
            piece = projected[:, p * PART : (p + 1) * PART]
            square = piece * piece
            mean = jnp.dot(square.astype(jnp.bfloat16), same, preferred_element_type=jnp.float32)
            pieces.append((piece * lax.rsqrt(mean + EPS_NORM)).astype(jnp.bfloat16))
        return jnp.concatenate(pieces, axis=1)

    def project(normed, which):
        return jnp.dot(normed, proj[which], preferred_element_type=jnp.float32)

    at = lax.broadcasted_iota(jnp.int32, (half, half), 1) - lax.broadcasted_iota(
        jnp.int32, (half, half), 0
    )
    bias[0] = jnp.where(at >= 0, 0.0, -1e30)
    bias[1] = jnp.where(at <= 0, 0.0, -1e30)

    def arrive(fill, own):
        if own:
            fill.wait()

    for own in (True, False):
        token_fills[0 if own else 1].wait()
        tokens_in = queries[...] if own else jnp.concatenate([halo[0], halo[1]], axis=0)
        arrive(weight_fills[0], own)
        pre_gate = apply(0, tokens_in)
        arrive(weight_fills[1], own)
        pre_up = apply(1, tokens_in)
        mixed = (pre_gate * jax.nn.sigmoid(pre_gate) * pre_up).astype(jnp.bfloat16)
        arrive(weight_fills[2], own)
        fast_out = apply(2, mixed)
        inverse = lax.rsqrt(jnp.mean(fast_out * fast_out, axis=1, keepdims=True) + EPS_NORM)
        normed = (fast_out * inverse * gain[...][None, :]).astype(jnp.bfloat16)
        for fill in proj_fills:
            arrive(fill, own)
        keys = head_norm(project(normed, proj_k))
        values = project(normed, proj_v).astype(jnp.bfloat16)
        if own:
            query_n[...] = head_norm(project(normed, proj_q))
            key_n[half : half + tokens, :] = keys
            value_b[half : half + tokens, :] = values
        else:
            key_n[0:half, :] = keys[:half]
            value_b[0:half, :] = values[:half]
            key_n[half + tokens :, :] = keys[half:]
            value_b[half + tokens :, :] = values[half:]

    for m in range(3):
        for p in range(features // WIDTH):
            wide[m, :, p * WIDTH : (p + 1) * WIDTH] = weights[m, p, col].astype(jnp.float32)
        stores[m].start()
    pair = 128 // size
    lane = lax.broadcasted_iota(jnp.int32, (half, 128), 1) // size
    ones = jnp.ones((3 * half, 128), jnp.bfloat16)

    for j in range(features // 128):
        lanes = pl.ds(j * 128, 128)
        for block in range(2):
            span = pl.ds(block * half, half)
            window = pl.ds(block * half, 3 * half)
            query = query_n[span, lanes]
            key = key_n[window, lanes]
            value = jnp.concatenate([value_b[window, lanes], ones], axis=1)
            result = jnp.zeros((half, 128), jnp.float32)
            for h in range(pair):
                scale = temper[j * pair + h] * (math.log2(math.e) / math.sqrt(size))
                scores = dot_rows(jnp.where(lane == h, query, jnp.zeros_like(query)), key)
                scores = jnp.concatenate(
                    [
                        scores[:, :half] + bias[0],
                        scores[:, half : 2 * half],
                        scores[:, 2 * half :] + bias[1],
                    ],
                    axis=1,
                )
                highest = jnp.max(scores, axis=1, keepdims=True)
                weight = jnp.exp2((scores - highest) * scale).astype(jnp.bfloat16)
                both = jnp.dot(weight, value, preferred_element_type=jnp.float32)
                result = jnp.where(lane == h, both[:, :128] / both[:, 128:], result)
            attended[span, lanes] = result.astype(jnp.bfloat16)
    for store in stores:
        store.wait()


def attend(n_col, queries, halo, weights, gain, proj_q, proj_k, proj_v, temper):
    tokens, features = queries.shape
    rows = weights.shape[2] // 3
    half = tokens // 2
    vmem, far = pl.BlockSpec(memory_space=VMEM), pl.BlockSpec(memory_space=pl.ANY)
    square = jax.ShapeDtypeStruct((rows, features), jnp.float32)
    return pl.pallas_call(
        functools.partial(attend_kernel, n_col, temper.shape[0]),
        out_shape=(jax.ShapeDtypeStruct((tokens, features), jnp.bfloat16), square, square, square),
        in_specs=[pl.BlockSpec(memory_space=pltpu.SMEM), far, far, far, vmem, far, far, far],
        out_specs=(vmem, far, far, far),
        scratch_shapes=[
            VMEM((tokens, features), jnp.bfloat16),
            VMEM((2, half, features), jnp.bfloat16),
            VMEM((3, features // WIDTH, n_col, rows, WIDTH), jnp.bfloat16),
            VMEM((3, features, features), jnp.bfloat16),
            VMEM((3, rows, features), jnp.float32),
            VMEM((tokens, features), jnp.bfloat16),
            VMEM((2 * tokens, features), jnp.bfloat16),
            VMEM((2 * tokens, features), jnp.bfloat16),
            VMEM((2, half, half), jnp.float32),
            pltpu.SemaphoreType.DMA((2,)),
            pltpu.SemaphoreType.DMA((3,)),
            pltpu.SemaphoreType.DMA((3,)),
            pltpu.SemaphoreType.DMA((3,)),
        ],
        compiler_params=pltpu.CompilerParams(vmem_limit_bytes=LIMIT),
        name="attend",
    )(temper, queries, halo, weights, gain, proj_q, proj_k, proj_v)


def per_device(
    n_row,
    n_col,
    token_keys,
    token_values,
    token_queries,
    step_rates,
    fast_gate,
    fast_up,
    fast_down,
    norm_gain,
    proj_query,
    proj_key,
    proj_value,
    head_temper,
):
    new, halo = update(
        n_row, n_col, fast_gate, fast_up, fast_down,
        token_keys, token_values, token_queries, step_rates,
    )
    return attend(
        n_col, token_queries, halo, new, norm_gain, proj_query, proj_key, proj_value, head_temper
    )


def solution(mesh):
    placed = (
        P(("row", "col"), None),
        P(("row", "col"), None),
        P(("row", "col"), None),
        P(("row", "col")),
        P("col", None),
        P("col", None),
        P("col", None),
        P(),
        P(),
        P(),
        P(),
        P(),
    )
    return jax.shard_map(
        functools.partial(per_device, mesh.shape["row"], mesh.shape["col"]),
        mesh=mesh,
        in_specs=placed,
        out_specs=(P(("row", "col"), None), P("col", None), P("col", None), P("col", None)),
        check_vma=False,
    )
```

```python
import functools
import math

import jax
import jax.numpy as jnp
from jax import lax
from jax.experimental import pallas as pl
from jax.experimental.pallas import tpu as pltpu
from jax.sharding import PartitionSpec as P

EPS_NORM = 1e-06
MESH = pl.DeviceIdType.MESH
VMEM = pltpu.VMEM
PART = 256
WIDTH = 128
ORDERS = ((1, 0, 3, 2), (3, 1, 2, 0), (0, 2, 1, 3), (0, 1, 2, 3), (1, 2, 3, 0), (2, 0, 1, 3))
LIMIT = 60 * 1024 * 1024


def dot_rows(left, right):
    return lax.dot_general(
        left, right, (((1,), (1,)), ((), ())), preferred_element_type=jnp.float32
    )


def update_kernel(
    n_row, n_col, bits,
    gate, up, down, keys_in, values_in, queries, rates,
    out_far, halo,
    out, fast, weights, keys, values, left, hidden, grads, held, from_col, *rest,
):
    landing, (
        total, f_sem, t_sem, x_sem, w_send, w_recv, h_send, h_recv,
        c_send, c_recv, r_send, r_recv, g_send, g_recv, o_send, o_recv,
    ) = rest[:bits], rest[bits:]
    row, col = lax.axis_index("row"), lax.axis_index("col")
    parts = grads.shape[0]
    unit = total.shape[0]
    rows = gate.shape[0]
    count = keys.shape[0]
    half = count // 2
    devices = n_row * n_col
    place = row * n_col + col
    after, before = lax.rem(place + 1, devices), lax.rem(place + devices - 1, devices)
    after_id = (after // n_col, lax.rem(after, n_col))
    before_id = (before // n_col, lax.rem(before, n_col))
    mine = [lax.rem(row // (1 << b), 2) for b in range(bits)]
    peers = [(row, lax.rem(col + step, n_col)) for step in range(1, n_col)]
    partners = [(row + (1 - 2 * mine[b]) * (1 << b), col) for b in range(bits)]

    barrier = pltpu.get_barrier_semaphore()
    everyone = peers + [after_id, before_id] + partners
    for target in everyone:
        pl.semaphore_signal(barrier, inc=1, device_id=target, device_id_type=MESH)
    fills = [
        pltpu.make_async_copy(source, fast.at[pl.ds(m * rows, rows)], f_sem.at[m])
        for m, source in enumerate((gate, up, down))
    ]
    tokens = [
        pltpu.make_async_copy(keys_in, keys, t_sem.at[0]),
        pltpu.make_async_copy(values_in, values, t_sem.at[1]),
    ]
    for copy in (fills[0], tokens[0], fills[1], fills[2], tokens[1]):
        copy.start()

    def remote(source, target, send, recv, device):
        copy = pltpu.make_async_remote_copy(
            src_ref=source, dst_ref=target, send_sem=send, recv_sem=recv,
            device_id=device, device_id_type=MESH,
        )
        copy.start()
        return copy

    given = {}
    for m in range(3):
        fills[m].wait()
        weights[m, col] = fast[m * rows : (m + 1) * rows, :].astype(jnp.bfloat16)
        if m == 0:
            pl.semaphore_wait(barrier, len(everyone))
        for step, peer in enumerate(peers):
            given[m, step] = remote(
                weights.at[m, col], weights.at[m, col], w_send.at[m, step], w_recv.at[m, step], peer
            )
    edges = {
        0: remote(queries.at[pl.ds(count - half, half)], halo.at[0], h_send.at[0], h_recv.at[0], after_id),
        1: remote(queries.at[pl.ds(0, half)], halo.at[1], h_send.at[1], h_recv.at[1], before_id),
    }

    def ready(m):
        for step in range(len(peers)):
            given[m, step].wait_recv()
        return weights[m].reshape(n_col * rows, weights.shape[3])

    for token in tokens:
        token.wait()
    token = keys[...]
    size = min(128, count)
    same = lax.broadcasted_iota(jnp.int32, (size, size), 0) == lax.broadcasted_iota(
        jnp.int32, (size, size), 1
    )
    rate_column = jnp.concatenate(
        [
            jnp.sum(
                jnp.where(same, rates[start : start + size][None, :], 0.0), axis=1, keepdims=True
            )
            for start in range(0, count, size)
        ],
        axis=0,
    )
    d_out = (-rate_column * values[...].astype(jnp.float32)).astype(jnp.bfloat16)
    left[2] = d_out.T
    pre_gate = dot_rows(token, ready(0))
    pre_up = dot_rows(token, ready(1))
    sig = jax.nn.sigmoid(pre_gate)
    silu = pre_gate * sig
    hidden[...] = (silu * pre_up).astype(jnp.bfloat16)
    d_hidden = jnp.dot(d_out, ready(2), preferred_element_type=jnp.float32)
    left[1] = (d_hidden * silu).astype(jnp.bfloat16).T
    left[0] = (d_hidden * pre_up * sig * (1.0 + pre_gate * (1.0 - sig))).astype(jnp.bfloat16).T

    def planes(fixed):
        return tuple(fixed.get(b, slice(None)) for b in reversed(range(bits)))

    free = min(3, bits)

    def order(p):
        if bits >= len(ORDERS[0]):
            return list(ORDERS[p % len(ORDERS)]) + list(range(len(ORDERS[0]), bits))
        return [(p + s) % free for s in range(free)] + list(range(free, bits))

    def chosen(p, steps):
        return {b: mine[b] for b in order(p)[:steps]}

    first, halvings = {}, {}

    def halve(p, s):
        b = order(p)[s]
        halvings[p, s] = remote(
            held.at[(p,) + planes({**chosen(p, s), b: 1 - mine[b]})],
            landing[s].at[p], r_send.at[p, s], r_recv.at[p, s], partners[b],
        )

    def gather_columns(p):
        for step in range(len(peers)):
            first[p, step].wait_recv()
        summed = grads[p, col].astype(jnp.float32)
        for step in range(len(peers)):
            summed = summed + from_col[step, p].astype(jnp.float32)
        for r in range(n_row):
            place_r = tuple((r >> b) & 1 for b in reversed(range(bits)))
            held[(p,) + place_r] = summed[r * unit : (r + 1) * unit, :].astype(jnp.bfloat16)
        halve(p, 0)

    joined = PART // WIDTH
    for start in range(0, parts, joined):
        for m, right in enumerate((keys, keys, hidden)):
            summed = jnp.dot(
                left[m], right[:, start * WIDTH : (start + joined) * WIDTH],
                preferred_element_type=jnp.float32,
            ).astype(jnp.bfloat16)
            for p in range(joined):
                for c in range(n_col):
                    grads[start + p, c, m * rows : (m + 1) * rows, :] = summed[
                        c * rows : (c + 1) * rows, p * WIDTH : (p + 1) * WIDTH
                    ]
        for p in range(start, start + joined):
            for step, peer in enumerate(peers):
                first[p, step] = remote(
                    grads.at[p, peer[1]], from_col.at[step, p],
                    c_send.at[p, step], c_recv.at[p, step], peer,
                )
        for p in range(start - joined, start):
            if p >= 0:
                gather_columns(p)
    for p in range(parts - joined, parts):
        gather_columns(p)
    for s in range(bits):
        for p in range(parts):
            halvings[p, s].wait_recv()
            index = (p,) + planes(chosen(p, s + 1))
            summed = held[index].astype(jnp.float32) + landing[s][p].astype(jnp.float32)
            if s < bits - 1:
                held[index] = summed.astype(jnp.bfloat16)
                halve(p, s + 1)
            else:
                total[:, p * WIDTH : (p + 1) * WIDTH] = summed

    if unit % 8 == 0:
        old = fast[pl.ds(pl.multiple_of(row * unit, 8), unit), :]
    else:
        old = sum(
            jnp.where(row == r, fast[r * unit : (r + 1) * unit, :], 0.0) for r in range(n_row)
        )
    moved = old - total[...]
    keep = jnp.sqrt(jnp.sum(old * old, axis=1, keepdims=True))
    new = moved * keep * lax.rsqrt(jnp.sum(moved * moved, axis=1, keepdims=True) + EPS_NORM)
    doublings, handed = {}, {}

    def double(p, s):
        part = (p, col) + planes(chosen(p, s + 1))
        doublings[p, s] = remote(
            out.at[part], out.at[part], g_send.at[p, s], g_recv.at[p, s], partners[order(p)[s]]
        )

    def hand(p, side, value):
        part = (p, col) + planes({order(p)[0]: value})
        for step, peer in enumerate(peers):
            handed[p, side, step] = remote(
                out.at[part], out.at[part], o_send.at[p, side, step], o_recv.at[p, side, step], peer
            )

    leaving = []

    def leave(p, step):
        giver = lax.rem(col + n_col - step, n_col)
        copy = pltpu.make_async_copy(out.at[p, giver], out_far.at[p, giver], x_sem.at[p, step])
        copy.start()
        leaving.append(copy)

    for p in range(parts):
        out[(p, col) + planes(chosen(p, bits))] = new[:, p * WIDTH : (p + 1) * WIDTH].astype(jnp.bfloat16)
        double(p, bits - 1)
    for s in reversed(range(bits)):
        for p in range(parts):
            doublings[p, s].wait_recv()
            if s > 0:
                double(p, s - 1)
            if s == 1:
                hand(p, 0, mine[order(p)[0]])
            if s == 0:
                hand(p, 1, 1 - mine[order(p)[0]])
                leave(p, 0)
    for p in range(parts):
        for step in range(len(peers)):
            for side in range(2):
                handed[p, side, step].wait_recv()
            leave(p, step + 1)
    for copy in edges.values():
        copy.wait_recv()
    for copy in leaving:
        copy.wait()
    for group in (given, edges, first, halvings, doublings, handed):
        for copy in group.values():
            copy.wait_send()


def update(n_row, n_col, gate, up, down, keys, values, queries, rates):
    rows, features = gate.shape
    tokens = keys.shape[0]
    parts = features // WIDTH
    stacked = 3 * rows
    bits = n_row.bit_length() - 1
    unit = stacked // n_row
    block = (2,) * bits + (unit, WIDTH)
    step = max(n_col - 1, 1)
    dma = pltpu.SemaphoreType.DMA
    landing = [VMEM((parts,) + (2,) * (bits - 1 - s) + (unit, WIDTH), jnp.bfloat16) for s in range(bits)]
    new, halo = pl.pallas_call(
        functools.partial(update_kernel, n_row, n_col, bits),
        out_shape=(
            jax.ShapeDtypeStruct((parts, n_col) + block, jnp.bfloat16),
            jax.ShapeDtypeStruct((2, tokens // 2, features), jnp.bfloat16),
        ),
        in_specs=[pl.BlockSpec(memory_space=pl.ANY)] * 6 + [pl.BlockSpec(memory_space=VMEM)],
        out_specs=(pl.BlockSpec(memory_space=pl.ANY), pl.BlockSpec(memory_space=pl.ANY)),
        scratch_shapes=[
            VMEM((parts, n_col) + block, jnp.bfloat16),
            VMEM((stacked, features), jnp.float32),
            VMEM((3, n_col, rows, features), jnp.bfloat16),
            VMEM((tokens, features), jnp.bfloat16),
            VMEM((tokens, features), jnp.bfloat16),
            VMEM((3, features, tokens), jnp.bfloat16),
            VMEM((tokens, features), jnp.bfloat16),
            VMEM((parts, n_col, stacked, WIDTH), jnp.bfloat16),
            VMEM((parts,) + block, jnp.bfloat16),
            VMEM((step, parts, stacked, WIDTH), jnp.bfloat16),
            *landing,
            VMEM((unit, features), jnp.float32),
            dma((3,)),
            dma((2,)),
            dma((parts, n_col)),
            dma((3, step)),
            dma((3, step)),
            dma((2,)),
            dma((2,)),
            dma((parts, step)),
            dma((parts, step)),
            dma((parts, bits)),
            dma((parts, bits)),
            dma((parts, bits)),
            dma((parts, bits)),
            dma((parts, 2, step)),
            dma((parts, 2, step)),
        ],
        compiler_params=pltpu.CompilerParams(
            collective_id=0, has_side_effects=True, vmem_limit_bytes=LIMIT
        ),
        cost_estimate=pl.CostEstimate(
            flops=12 * tokens * features * features, bytes_accessed=12 * 2**20, transcendentals=0
        ),
        name="update",
    )(gate, up, down, keys, values, queries, rates)
    return new.reshape(parts, n_col, stacked, WIDTH), halo


def attend_kernel(
    n_col, heads, temper, queries_in, halo_in, weights_in, gain, proj_q_in, proj_k_in, proj_v_in,
    attended, new_gate, new_up, new_down,
    queries, halo, weights, proj, wide, query_n, key_n, value_b, bias, in_sem, w_sem, p_sem, n_sem,
):
    rows = weights.shape[3]
    tokens, features = queries.shape
    parts = features // PART
    joined = PART // WIDTH
    half = tokens // 2
    size = features // heads
    col = lax.axis_index("col")
    proj_q, proj_k, proj_v = 0, 1, 2
    token_fills = [
        pltpu.make_async_copy(queries_in, queries, in_sem.at[0]),
        pltpu.make_async_copy(halo_in, halo, in_sem.at[1]),
    ]
    weight_fills = [
        pltpu.make_async_copy(
            weights_in.at[:, :, pl.ds(m * rows, rows), :], weights.at[m], w_sem.at[m]
        )
        for m in range(3)
    ]
    proj_fills = [
        pltpu.make_async_copy(source, proj.at[i], p_sem.at[i])
        for i, source in enumerate((proj_q_in, proj_k_in, proj_v_in))
    ]
    for fill in (
        token_fills[0], *weight_fills, proj_fills[1], proj_fills[2], proj_fills[0], token_fills[1]
    ):
        fill.start()
    stores = [
        pltpu.make_async_copy(wide.at[m], target, n_sem.at[m])
        for m, target in enumerate((new_gate, new_up, new_down))
    ]

    def whole(m, p):
        return jnp.concatenate(
            [
                jnp.concatenate([weights[m, p * joined + i, c] for i in range(joined)], axis=1)
                for c in range(n_col)
            ],
            axis=0,
        )

    def apply(m, left):
        return sum(dot_rows(left[:, p * PART : (p + 1) * PART], whole(m, p)) for p in range(parts))

    group_r = lax.broadcasted_iota(jnp.int32, (PART, PART), 0) // size
    group_c = lax.broadcasted_iota(jnp.int32, (PART, PART), 1) // size
    same = jnp.where(group_r == group_c, 1.0 / size, 0.0).astype(jnp.bfloat16)

    def head_norm(projected):
        pieces = []
        for p in range(parts):
            piece = projected[:, p * PART : (p + 1) * PART]
            square = piece * piece
            mean = jnp.dot(square.astype(jnp.bfloat16), same, preferred_element_type=jnp.float32)
            pieces.append((piece * lax.rsqrt(mean + EPS_NORM)).astype(jnp.bfloat16))
        return jnp.concatenate(pieces, axis=1)

    def project(normed, which):
        return jnp.dot(normed, proj[which], preferred_element_type=jnp.float32)

    at = lax.broadcasted_iota(jnp.int32, (half, half), 1) - lax.broadcasted_iota(
        jnp.int32, (half, half), 0
    )
    bias[0] = jnp.where(at <= 0, 0.0, -1e30)
    bias[1] = jnp.where(at >= 0, 0.0, -1e30)

    def arrive(fill, own):
        if own:
            fill.wait()

    for own in (True, False):
        token_fills[0 if own else 1].wait()
        tokens_in = queries[...] if own else jnp.concatenate([halo[0], halo[1]], axis=0)
        arrive(weight_fills[0], own)
        pre_gate = apply(0, tokens_in)
        arrive(weight_fills[1], own)
        pre_up = apply(1, tokens_in)
        mixed = (pre_gate * jax.nn.sigmoid(pre_gate) * pre_up).astype(jnp.bfloat16)
        arrive(weight_fills[2], own)
        fast_out = apply(2, mixed)
        inverse = lax.rsqrt(jnp.mean(fast_out * fast_out, axis=1, keepdims=True) + EPS_NORM)
        normed = (fast_out * inverse * gain[...][None, :]).astype(jnp.bfloat16)
        for fill in proj_fills:
            arrive(fill, own)
        keys = head_norm(project(normed, proj_k))
        values = project(normed, proj_v).astype(jnp.bfloat16).T
        if own:
            query_n[...] = head_norm(project(normed, proj_q))
            key_n[half : half + tokens, :] = keys
            value_b[:, half : half + tokens] = values
        else:
            key_n[0:half, :] = keys[:half]
            value_b[:, 0:half] = values[:, :half]
            key_n[half + tokens :, :] = keys[half:]
            value_b[:, half + tokens :] = values[:, half:]

    for m in range(3):
        for p in range(features // WIDTH):
            wide[m, :, p * WIDTH : (p + 1) * WIDTH] = weights[m, p, col].astype(jnp.float32)
        stores[m].start()
    pair = 128 // size
    lane = lax.broadcasted_iota(jnp.int32, (half, 128), 1) // size
    ones = jnp.ones((16, 3 * half), jnp.bfloat16)
    for j in range(features // 128):
        lanes = pl.ds(j * 128, 128)
        for block in range(2):
            span = pl.ds(block * half, half)
            window = pl.ds(block * half, 3 * half)
            query = query_n[span, lanes]
            key = key_n[window, lanes]
            turned = []
            for h in range(pair):
                head = j * pair + h
                scale = temper[head] * (math.log2(math.e) / math.sqrt(size))
                scores = dot_rows(key, jnp.where(lane == h, query, jnp.zeros_like(query)))
                scores = jnp.concatenate(
                    [
                        scores[:half] + bias[0],
                        scores[half : 2 * half],
                        scores[2 * half :] + bias[1],
                    ],
                    axis=0,
                )
                highest = jnp.max(scores, axis=0, keepdims=True)
                weight = jnp.exp2((scores - highest) * scale).astype(jnp.bfloat16)
                value = jnp.concatenate(
                    [value_b[head * size : (head + 1) * size, window], ones], axis=0
                )
                both = jnp.dot(value, weight, preferred_element_type=jnp.float32)
                turned.append(both[:size] / both[size : size + 1])
            attended[span, lanes] = jnp.concatenate(turned, axis=0).T.astype(jnp.bfloat16)
    for store in stores:
        store.wait()


def attend(n_col, queries, halo, weights, gain, proj_q, proj_k, proj_v, temper):
    tokens, features = queries.shape
    rows = weights.shape[2] // 3
    half = tokens // 2
    vmem, far = pl.BlockSpec(memory_space=VMEM), pl.BlockSpec(memory_space=pl.ANY)
    square = jax.ShapeDtypeStruct((rows, features), jnp.float32)
    return pl.pallas_call(
        functools.partial(attend_kernel, n_col, temper.shape[0]),
        out_shape=(jax.ShapeDtypeStruct((tokens, features), jnp.bfloat16), square, square, square),
        in_specs=[pl.BlockSpec(memory_space=pltpu.SMEM), far, far, far, vmem, far, far, far],
        out_specs=(vmem, far, far, far),
        scratch_shapes=[
            VMEM((tokens, features), jnp.bfloat16),
            VMEM((2, half, features), jnp.bfloat16),
            VMEM((3, features // WIDTH, n_col, rows, WIDTH), jnp.bfloat16),
            VMEM((3, features, features), jnp.bfloat16),
            VMEM((3, rows, features), jnp.float32),
            VMEM((tokens, features), jnp.bfloat16),
            VMEM((2 * tokens, features), jnp.bfloat16),
            VMEM((features, 2 * tokens), jnp.bfloat16),
            VMEM((2, half, half), jnp.float32),
            pltpu.SemaphoreType.DMA((2,)),
            pltpu.SemaphoreType.DMA((3,)),
            pltpu.SemaphoreType.DMA((3,)),
            pltpu.SemaphoreType.DMA((3,)),
        ],
        compiler_params=pltpu.CompilerParams(vmem_limit_bytes=LIMIT),
        name="attend",
    )(temper, queries, halo, weights, gain, proj_q, proj_k, proj_v)


def per_device(
    n_row,
    n_col,
    token_keys,
    token_values,
    token_queries,
    step_rates,
    fast_gate,
    fast_up,
    fast_down,
    norm_gain,
    proj_query,
    proj_key,
    proj_value,
    head_temper,
):
    new, halo = update(
        n_row, n_col, fast_gate, fast_up, fast_down,
        token_keys, token_values, token_queries, step_rates,
    )
    return attend(
        n_col, token_queries, halo, new, norm_gain, proj_query, proj_key, proj_value, head_temper
    )


def solution(mesh):
    placed = (
        P(("row", "col"), None),
        P(("row", "col"), None),
        P(("row", "col"), None),
        P(("row", "col")),
        P("col", None),
        P("col", None),
        P("col", None),
        P(),
        P(),
        P(),
        P(),
        P(),
    )
    return jax.shard_map(
        functools.partial(per_device, mesh.shape["row"], mesh.shape["col"]),
        mesh=mesh,
        in_specs=placed,
        out_specs=(P(("row", "col"), None), P("col", None), P("col", None), P("col", None)),
        check_vma=False,
    )
```

```python
import functools
import math

import jax
import jax.numpy as jnp
from jax import lax
from jax.experimental import pallas as pl
from jax.experimental.pallas import tpu as pltpu
from jax.sharding import PartitionSpec as P

EPS_NORM = 1e-06
MESH = pl.DeviceIdType.MESH
VMEM = pltpu.VMEM
PART = 256
WIDTH = 128
LIMIT = 60 * 1024 * 1024


def dot_rows(left, right):
    return lax.dot_general(
        left, right, (((1,), (1,)), ((), ())), preferred_element_type=jnp.float32
    )


def update_kernel(
    n_row, n_col, bits,
    gate, up, down, keys_in, values_in, queries, rates,
    out_far, halo,
    out, fast, weights, keys, values, left, hidden, grads, held, from_col, *rest,
):
    landing, (
        total, f_sem, t_sem, x_sem, w_send, w_recv, h_send, h_recv,
        c_send, c_recv, r_send, r_recv, g_send, g_recv, o_send, o_recv,
    ) = rest[:bits], rest[bits:]
    row, col = lax.axis_index("row"), lax.axis_index("col")
    parts = grads.shape[0]
    unit = total.shape[0]
    rows = gate.shape[0]
    count = keys.shape[0]
    half = count // 2
    devices = n_row * n_col
    place = row * n_col + col
    after, before = lax.rem(place + 1, devices), lax.rem(place + devices - 1, devices)
    after_id = (after // n_col, lax.rem(after, n_col))
    before_id = (before // n_col, lax.rem(before, n_col))
    mine = [lax.rem(row // (1 << b), 2) for b in range(bits)]
    peers = [(row, lax.rem(col + step, n_col)) for step in range(1, n_col)]
    partners = [(row + (1 - 2 * mine[b]) * (1 << b), col) for b in range(bits)]

    barrier = pltpu.get_barrier_semaphore()
    everyone = peers + [after_id, before_id] + partners
    for target in everyone:
        pl.semaphore_signal(barrier, inc=1, device_id=target, device_id_type=MESH)
    fills = [
        pltpu.make_async_copy(source, fast.at[pl.ds(m * rows, rows)], f_sem.at[m])
        for m, source in enumerate((gate, up, down))
    ]
    tokens = [
        pltpu.make_async_copy(keys_in, keys, t_sem.at[0]),
        pltpu.make_async_copy(values_in, values, t_sem.at[1]),
    ]
    for copy in (fills[0], tokens[0], fills[1], fills[2], tokens[1]):
        copy.start()

    def remote(source, target, send, recv, device):
        copy = pltpu.make_async_remote_copy(
            src_ref=source, dst_ref=target, send_sem=send, recv_sem=recv,
            device_id=device, device_id_type=MESH,
        )
        copy.start()
        return copy

    given = {}
    for m in range(3):
        fills[m].wait()
        weights[m, col] = fast[m * rows : (m + 1) * rows, :].astype(jnp.bfloat16)
        if m == 0:
            pl.semaphore_wait(barrier, len(everyone))
        for step, peer in enumerate(peers):
            given[m, step] = remote(
                weights.at[m, col], weights.at[m, col], w_send.at[m, step], w_recv.at[m, step], peer
            )
    edges = {
        0: remote(queries.at[pl.ds(count - half, half)], halo.at[0], h_send.at[0], h_recv.at[0], after_id),
        1: remote(queries.at[pl.ds(0, half)], halo.at[1], h_send.at[1], h_recv.at[1], before_id),
    }

    def ready(m):
        for step in range(len(peers)):
            given[m, step].wait_recv()
        return weights[m].reshape(n_col * rows, weights.shape[3])

    for token in tokens:
        token.wait()
    token = keys[...]
    size = min(128, count)
    same = lax.broadcasted_iota(jnp.int32, (size, size), 0) == lax.broadcasted_iota(
        jnp.int32, (size, size), 1
    )
    rate_column = jnp.concatenate(
        [
            jnp.sum(
                jnp.where(same, rates[start : start + size][None, :], 0.0), axis=1, keepdims=True
            )
            for start in range(0, count, size)
        ],
        axis=0,
    )
    d_out = (-rate_column * values[...].astype(jnp.float32)).astype(jnp.bfloat16)
    left[2] = d_out.T
    pre_gate = dot_rows(token, ready(0))
    pre_up = dot_rows(token, ready(1))
    sig = jax.nn.sigmoid(pre_gate)
    silu = pre_gate * sig
    hidden[...] = (silu * pre_up).astype(jnp.bfloat16)
    d_hidden = jnp.dot(d_out, ready(2), preferred_element_type=jnp.float32)
    left[1] = (d_hidden * silu).astype(jnp.bfloat16).T
    left[0] = (d_hidden * pre_up * sig * (1.0 + pre_gate * (1.0 - sig))).astype(jnp.bfloat16).T

    def planes(fixed):
        return tuple(fixed.get(b, slice(None)) for b in reversed(range(bits)))

    free = min(3, bits)

    def order(p):
        return [(p + s) % free for s in range(free)] + list(range(free, bits))

    def chosen(p, steps):
        return {b: mine[b] for b in order(p)[:steps]}

    first, halvings = {}, {}

    def halve(p, s):
        b = order(p)[s]
        halvings[p, s] = remote(
            held.at[(p,) + planes({**chosen(p, s), b: 1 - mine[b]})],
            landing[s].at[p], r_send.at[p, s], r_recv.at[p, s], partners[b],
        )

    def gather_columns(p):
        for step in range(len(peers)):
            first[p, step].wait_recv()
        summed = grads[p, col].astype(jnp.float32)
        for step in range(len(peers)):
            summed = summed + from_col[step, p].astype(jnp.float32)
        for r in range(n_row):
            place_r = tuple((r >> b) & 1 for b in reversed(range(bits)))
            held[(p,) + place_r] = summed[r * unit : (r + 1) * unit, :].astype(jnp.bfloat16)
        halve(p, 0)

    joined = PART // WIDTH
    for start in range(0, parts, joined):
        for m, right in enumerate((keys, keys, hidden)):
            summed = jnp.dot(
                left[m], right[:, start * WIDTH : (start + joined) * WIDTH],
                preferred_element_type=jnp.float32,
            ).astype(jnp.bfloat16)
            for p in range(joined):
                for c in range(n_col):
                    grads[start + p, c, m * rows : (m + 1) * rows, :] = summed[
                        c * rows : (c + 1) * rows, p * WIDTH : (p + 1) * WIDTH
                    ]
        for p in range(start, start + joined):
            for step, peer in enumerate(peers):
                first[p, step] = remote(
                    grads.at[p, peer[1]], from_col.at[step, p],
                    c_send.at[p, step], c_recv.at[p, step], peer,
                )
        for p in range(start - joined, start):
            if p >= 0:
                gather_columns(p)
    for p in range(parts - joined, parts):
        gather_columns(p)
    for s in range(bits):
        for p in range(parts):
            halvings[p, s].wait_recv()
            index = (p,) + planes(chosen(p, s + 1))
            summed = held[index].astype(jnp.float32) + landing[s][p].astype(jnp.float32)
            if s < bits - 1:
                held[index] = summed.astype(jnp.bfloat16)
                halve(p, s + 1)
            else:
                total[:, p * WIDTH : (p + 1) * WIDTH] = summed

    if unit % 8 == 0:
        old = fast[pl.ds(pl.multiple_of(row * unit, 8), unit), :]
    else:
        old = sum(
            jnp.where(row == r, fast[r * unit : (r + 1) * unit, :], 0.0) for r in range(n_row)
        )
    moved = old - total[...]
    keep = jnp.sqrt(jnp.sum(old * old, axis=1, keepdims=True))
    new = moved * keep * lax.rsqrt(jnp.sum(moved * moved, axis=1, keepdims=True) + EPS_NORM)
    doublings, handed = {}, {}

    def double(p, s):
        part = (p, col) + planes(chosen(p, s + 1))
        doublings[p, s] = remote(
            out.at[part], out.at[part], g_send.at[p, s], g_recv.at[p, s], partners[order(p)[s]]
        )

    def hand(p, side, value):
        part = (p, col) + planes({order(p)[0]: value})
        for step, peer in enumerate(peers):
            handed[p, side, step] = remote(
                out.at[part], out.at[part], o_send.at[p, side, step], o_recv.at[p, side, step], peer
            )

    leaving = []

    def leave(p, step):
        giver = lax.rem(col + n_col - step, n_col)
        copy = pltpu.make_async_copy(out.at[p, giver], out_far.at[p, giver], x_sem.at[p, step])
        copy.start()
        leaving.append(copy)

    for p in range(parts):
        out[(p, col) + planes(chosen(p, bits))] = new[:, p * WIDTH : (p + 1) * WIDTH].astype(jnp.bfloat16)
        double(p, bits - 1)
    for s in reversed(range(bits)):
        for p in range(parts):
            doublings[p, s].wait_recv()
            if s > 0:
                double(p, s - 1)
            if s == 1:
                hand(p, 0, mine[order(p)[0]])
            if s == 0:
                hand(p, 1, 1 - mine[order(p)[0]])
                leave(p, 0)
    for p in range(parts):
        for step in range(len(peers)):
            for side in range(2):
                handed[p, side, step].wait_recv()
            leave(p, step + 1)
    for copy in edges.values():
        copy.wait_recv()
    for copy in leaving:
        copy.wait()
    for group in (given, edges, first, halvings, doublings, handed):
        for copy in group.values():
            copy.wait_send()


def update(n_row, n_col, gate, up, down, keys, values, queries, rates):
    rows, features = gate.shape
    tokens = keys.shape[0]
    parts = features // WIDTH
    stacked = 3 * rows
    bits = n_row.bit_length() - 1
    unit = stacked // n_row
    block = (2,) * bits + (unit, WIDTH)
    step = max(n_col - 1, 1)
    dma = pltpu.SemaphoreType.DMA
    landing = [VMEM((parts,) + (2,) * (bits - 1 - s) + (unit, WIDTH), jnp.bfloat16) for s in range(bits)]
    new, halo = pl.pallas_call(
        functools.partial(update_kernel, n_row, n_col, bits),
        out_shape=(
            jax.ShapeDtypeStruct((parts, n_col) + block, jnp.bfloat16),
            jax.ShapeDtypeStruct((2, tokens // 2, features), jnp.bfloat16),
        ),
        in_specs=[pl.BlockSpec(memory_space=pl.ANY)] * 6 + [pl.BlockSpec(memory_space=VMEM)],
        out_specs=(pl.BlockSpec(memory_space=pl.ANY), pl.BlockSpec(memory_space=pl.ANY)),
        scratch_shapes=[
            VMEM((parts, n_col) + block, jnp.bfloat16),
            VMEM((stacked, features), jnp.float32),
            VMEM((3, n_col, rows, features), jnp.bfloat16),
            VMEM((tokens, features), jnp.bfloat16),
            VMEM((tokens, features), jnp.bfloat16),
            VMEM((3, features, tokens), jnp.bfloat16),
            VMEM((tokens, features), jnp.bfloat16),
            VMEM((parts, n_col, stacked, WIDTH), jnp.bfloat16),
            VMEM((parts,) + block, jnp.bfloat16),
            VMEM((step, parts, stacked, WIDTH), jnp.bfloat16),
            *landing,
            VMEM((unit, features), jnp.float32),
            dma((3,)),
            dma((2,)),
            dma((parts, n_col)),
            dma((3, step)),
            dma((3, step)),
            dma((2,)),
            dma((2,)),
            dma((parts, step)),
            dma((parts, step)),
            dma((parts, bits)),
            dma((parts, bits)),
            dma((parts, bits)),
            dma((parts, bits)),
            dma((parts, 2, step)),
            dma((parts, 2, step)),
        ],
        compiler_params=pltpu.CompilerParams(
            collective_id=0, has_side_effects=True, vmem_limit_bytes=LIMIT
        ),
        cost_estimate=pl.CostEstimate(
            flops=12 * tokens * features * features, bytes_accessed=12 * 2**20, transcendentals=0
        ),
        name="update",
    )(gate, up, down, keys, values, queries, rates)
    return new.reshape(parts, n_col, stacked, WIDTH), halo


def attend_kernel(
    n_col, heads, temper, queries_in, halo_in, weights_in, gain, proj_q_in, proj_k_in, proj_v_in,
    attended, new_gate, new_up, new_down,
    queries, halo, weights, proj, wide, query_n, key_n, value_b, bias, in_sem, w_sem, p_sem, n_sem,
):
    rows = weights.shape[3]
    tokens, features = queries.shape
    parts = features // PART
    joined = PART // WIDTH
    half = tokens // 2
    size = features // heads
    col = lax.axis_index("col")
    proj_q, proj_k, proj_v = 0, 1, 2
    token_fills = [
        pltpu.make_async_copy(queries_in, queries, in_sem.at[0]),
        pltpu.make_async_copy(halo_in, halo, in_sem.at[1]),
    ]
    weight_fills = [
        pltpu.make_async_copy(
            weights_in.at[:, :, pl.ds(m * rows, rows), :], weights.at[m], w_sem.at[m]
        )
        for m in range(3)
    ]
    proj_fills = [
        pltpu.make_async_copy(source, proj.at[i], p_sem.at[i])
        for i, source in enumerate((proj_q_in, proj_k_in, proj_v_in))
    ]
    for fill in (
        token_fills[0], *weight_fills, proj_fills[1], proj_fills[2], proj_fills[0], token_fills[1]
    ):
        fill.start()
    stores = [
        pltpu.make_async_copy(wide.at[m], target, n_sem.at[m])
        for m, target in enumerate((new_gate, new_up, new_down))
    ]

    def whole(m, p):
        return jnp.concatenate(
            [
                jnp.concatenate([weights[m, p * joined + i, c] for i in range(joined)], axis=1)
                for c in range(n_col)
            ],
            axis=0,
        )

    def apply(m, left):
        return sum(dot_rows(left[:, p * PART : (p + 1) * PART], whole(m, p)) for p in range(parts))

    group_r = lax.broadcasted_iota(jnp.int32, (PART, PART), 0) // size
    group_c = lax.broadcasted_iota(jnp.int32, (PART, PART), 1) // size
    same = jnp.where(group_r == group_c, 1.0 / size, 0.0).astype(jnp.bfloat16)

    def head_norm(projected):
        pieces = []
        for p in range(parts):
            piece = projected[:, p * PART : (p + 1) * PART]
            square = piece * piece
            mean = jnp.dot(square.astype(jnp.bfloat16), same, preferred_element_type=jnp.float32)
            pieces.append((piece * lax.rsqrt(mean + EPS_NORM)).astype(jnp.bfloat16))
        return jnp.concatenate(pieces, axis=1)

    def project(normed, which):
        return jnp.dot(normed, proj[which], preferred_element_type=jnp.float32)

    at = lax.broadcasted_iota(jnp.int32, (half, half), 1) - lax.broadcasted_iota(
        jnp.int32, (half, half), 0
    )
    bias[0] = jnp.where(at >= 0, 0.0, -1e30)
    bias[1] = jnp.where(at <= 0, 0.0, -1e30)

    def arrive(fill, own):
        if own:
            fill.wait()

    for own in (True, False):
        token_fills[0 if own else 1].wait()
        tokens_in = queries[...] if own else jnp.concatenate([halo[0], halo[1]], axis=0)
        arrive(weight_fills[0], own)
        pre_gate = apply(0, tokens_in)
        arrive(weight_fills[1], own)
        pre_up = apply(1, tokens_in)
        mixed = (pre_gate * jax.nn.sigmoid(pre_gate) * pre_up).astype(jnp.bfloat16)
        arrive(weight_fills[2], own)
        fast_out = apply(2, mixed)
        inverse = lax.rsqrt(jnp.mean(fast_out * fast_out, axis=1, keepdims=True) + EPS_NORM)
        normed = (fast_out * inverse * gain[...][None, :]).astype(jnp.bfloat16)
        for fill in proj_fills:
            arrive(fill, own)
        keys = head_norm(project(normed, proj_k))
        values = project(normed, proj_v).astype(jnp.bfloat16)
        if own:
            query_n[...] = head_norm(project(normed, proj_q))
            key_n[half : half + tokens, :] = keys
            value_b[half : half + tokens, :] = values
        else:
            key_n[0:half, :] = keys[:half]
            value_b[0:half, :] = values[:half]
            key_n[half + tokens :, :] = keys[half:]
            value_b[half + tokens :, :] = values[half:]

    for m in range(3):
        for p in range(features // WIDTH):
            wide[m, :, p * WIDTH : (p + 1) * WIDTH] = weights[m, p, col].astype(jnp.float32)
        stores[m].start()
    pair = 128 // size
    lane = lax.broadcasted_iota(jnp.int32, (half, 128), 1) // size
    ones = jnp.ones((3 * half, 128), jnp.bfloat16)

    tasks = [(j, block) for j in range(features // 128) for block in range(2)]

    def score(j, block):
        lanes = pl.ds(j * 128, 128)
        query = query_n[pl.ds(block * half, half), lanes]
        stacked = jnp.concatenate(
            [jnp.where(lane == h, query, jnp.zeros_like(query)) for h in range(pair)], axis=0
        )
        return dot_rows(stacked, key_n[pl.ds(block * half, 3 * half), lanes])

    def soften(j, scores):
        weights_b = []
        for h in range(pair):
            scale = temper[j * pair + h] * (math.log2(math.e) / math.sqrt(size))
            mine = scores[h * half : (h + 1) * half]
            mine = jnp.concatenate(
                [
                    mine[:, :half] + bias[0],
                    mine[:, half : 2 * half],
                    mine[:, 2 * half :] + bias[1],
                ],
                axis=1,
            )
            highest = jnp.max(mine, axis=1, keepdims=True)
            weights_b.append(jnp.exp2((mine - highest) * scale).astype(jnp.bfloat16))
        return jnp.concatenate(weights_b, axis=0)

    def finish(j, block, weight):
        lanes = pl.ds(j * 128, 128)
        value = jnp.concatenate([value_b[pl.ds(block * half, 3 * half), lanes], ones], axis=1)
        both = jnp.dot(weight, value, preferred_element_type=jnp.float32)
        result = jnp.zeros((half, 128), jnp.float32)
        for h in range(pair):
            mine = both[h * half : (h + 1) * half]
            result = jnp.where(lane == h, mine[:, :128] / mine[:, 128:], result)
        attended[pl.ds(block * half, half), lanes] = result.astype(jnp.bfloat16)

    ahead = score(*tasks[0])
    for i, (j, block) in enumerate(tasks):
        scores = ahead
        if i + 1 < len(tasks):
            ahead = score(*tasks[i + 1])
        finish(j, block, soften(j, scores))
    for store in stores:
        store.wait()


def attend(n_col, queries, halo, weights, gain, proj_q, proj_k, proj_v, temper):
    tokens, features = queries.shape
    rows = weights.shape[2] // 3
    half = tokens // 2
    vmem, far = pl.BlockSpec(memory_space=VMEM), pl.BlockSpec(memory_space=pl.ANY)
    square = jax.ShapeDtypeStruct((rows, features), jnp.float32)
    return pl.pallas_call(
        functools.partial(attend_kernel, n_col, temper.shape[0]),
        out_shape=(jax.ShapeDtypeStruct((tokens, features), jnp.bfloat16), square, square, square),
        in_specs=[pl.BlockSpec(memory_space=pltpu.SMEM), far, far, far, vmem, far, far, far],
        out_specs=(vmem, far, far, far),
        scratch_shapes=[
            VMEM((tokens, features), jnp.bfloat16),
            VMEM((2, half, features), jnp.bfloat16),
            VMEM((3, features // WIDTH, n_col, rows, WIDTH), jnp.bfloat16),
            VMEM((3, features, features), jnp.bfloat16),
            VMEM((3, rows, features), jnp.float32),
            VMEM((tokens, features), jnp.bfloat16),
            VMEM((2 * tokens, features), jnp.bfloat16),
            VMEM((2 * tokens, features), jnp.bfloat16),
            VMEM((2, half, half), jnp.float32),
            pltpu.SemaphoreType.DMA((2,)),
            pltpu.SemaphoreType.DMA((3,)),
            pltpu.SemaphoreType.DMA((3,)),
            pltpu.SemaphoreType.DMA((3,)),
        ],
        compiler_params=pltpu.CompilerParams(vmem_limit_bytes=LIMIT),
        name="attend",
    )(temper, queries, halo, weights, gain, proj_q, proj_k, proj_v)


def per_device(
    n_row,
    n_col,
    token_keys,
    token_values,
    token_queries,
    step_rates,
    fast_gate,
    fast_up,
    fast_down,
    norm_gain,
    proj_query,
    proj_key,
    proj_value,
    head_temper,
):
    new, halo = update(
        n_row, n_col, fast_gate, fast_up, fast_down,
        token_keys, token_values, token_queries, step_rates,
    )
    return attend(
        n_col, token_queries, halo, new, norm_gain, proj_query, proj_key, proj_value, head_temper
    )


def solution(mesh):
    placed = (
        P(("row", "col"), None),
        P(("row", "col"), None),
        P(("row", "col"), None),
        P(("row", "col")),
        P("col", None),
        P("col", None),
        P("col", None),
        P(),
        P(),
        P(),
        P(),
        P(),
    )
    return jax.shard_map(
        functools.partial(per_device, mesh.shape["row"], mesh.shape["col"]),
        mesh=mesh,
        in_specs=placed,
        out_specs=(P(("row", "col"), None), P("col", None), P("col", None), P("col", None)),
        check_vma=False,
    )
```
